32 devices in a mesh: groups: 2 (over x), weight: 16 (over z, y, core).
Axes of the slice: x: 2, y: 2, z: 4, core: 2. Of those that a mesh axis runs over, the one named last changes fastest.
Arguments:
- hidden_in: bfloat16 [512, 8192], P('groups', 'weight'), parts along dimension 0, may hold values from -500 to 500
- norm_gain: bfloat16 [1, 8192], P(None, 'weight'), may hold values from 0.099609375 to 1.8984375
- w_query: bfloat16 [8192, 4096], P(None, 'weight'), may hold values from -1 to 1
- w_key: bfloat16 [8192, 512], P(None, 'weight'), may hold values from -8 to 8
- w_value: bfloat16 [8192, 512], P(None, 'weight'), may hold values from -0.0625 to 0.0625
- w_out: bfloat16 [4096, 8192], P(None, 'weight'), may hold values from -0.09375 to 0.09375
- cache_keys: bfloat16 [24576, 4, 128], P(('groups', 'weight')), parts along dimension 0, may hold values from -200 to 200
- cache_values: bfloat16 [24576, 4, 128], P(('groups', 'weight')), parts along dimension 0, may hold values from -6 to 6
- offset: int32 [2], P('groups'), parts along dimension 0, may hold values from 11904 to 12288
- length: int32 [2], P('groups'), parts along dimension 0, may hold values from 12288 to 12544
Outputs:
- attn_branch: bfloat16 [512, 8192], P('groups', 'weight'), parts along dimension 0
The draws below stay inside these ranges and needn't reach their ends.
There are 2 independent parts, one for each index of `groups`. The reference program is written for one: setup_inputs(seed, part) draws one part's arguments, and reference() takes and returns one part's arrays. A program takes and returns all parts, laid end to end along the dimension named above; an argument that names none is the same for every part. Nothing has to cross between parts.
All inputs are finite; a program needn't handle non-finite values.
Results may differ from the reference program's by a relative error of at most 0.017.
The reference program's roundings to bfloat16 on the way count: a program that leaves them out, or rounds other values in their place, can miss the bound.
Values may be sent and summed in bfloat16 or wider, within the bound.
A program may use at most 128 MiB of HBM per device.

```python
import math
import jax
import jax.numpy as jnp
from jax import lax

MODEL_DIM = 8192
QHEADS = 32
KVHEADS = 4
HEAD_DIM = 128
NEW_TOKENS = 256
CACHE_DEV = 768
CONTEXT = 12288


def draw_hidden_in(key, part):
    key = jax.random.fold_in(key, 3)
    key_rows, key_cols, key_base = jax.random.split(key, 3)
    row_scale = jnp.exp(jax.random.uniform(key_rows, (NEW_TOKENS, 1), jnp.float32, 0.0, math.log(10.0)))
    col_scale = jnp.exp(jax.random.uniform(key_cols, (1, MODEL_DIM), jnp.float32, 0.0, math.log(10.0)))
    base = jnp.clip(jax.random.normal(key_base, (NEW_TOKENS, MODEL_DIM), jnp.float32), -4.0, 4.0)
    return (base * row_scale * col_scale).astype(jnp.bfloat16)


def draw_w_query(key, part):
    key = jax.random.fold_in(key, 11)
    key_order, key_base = jax.random.split(key, 2)
    levels = 0.7 * 5.0 ** (jnp.arange(KVHEADS, dtype=jnp.float32) / (KVHEADS - 1))
    order = jax.random.permutation(key_order, KVHEADS)
    group_scale = levels[order]
    head_scale = jnp.repeat(group_scale, QHEADS // KVHEADS)
    base = jnp.clip(jax.random.normal(key_base, (MODEL_DIM, QHEADS, HEAD_DIM), jnp.float32), -4.0, 4.0)
    scaled = base * head_scale[None, :, None] * MODEL_DIM ** (-0.5)
    return scaled.reshape(MODEL_DIM, QHEADS * HEAD_DIM).astype(jnp.bfloat16)


def draw_w_key(key, part):
    key = jax.random.fold_in(key, 5)
    base = jnp.clip(jax.random.normal(key, (MODEL_DIM, KVHEADS * HEAD_DIM), jnp.float32), -4.0, 4.0)
    return (base * 40.0 * MODEL_DIM ** (-0.5)).astype(jnp.bfloat16)


def draw_cache_keys(key, part):
    key = jax.random.fold_in(key, 7)
    key_base = jax.random.fold_in(key, 0)
    base = jnp.clip(jax.random.normal(key_base, (CONTEXT, KVHEADS, HEAD_DIM), jnp.float32), -5.0, 5.0)
    return (base * 40.0).astype(jnp.bfloat16)


def steps_of(rng, dims, pieces, smallest, top_value):
    factor_of, own = 1.0, jax.random.fold_in(rng, 6)
    for axis_at, parts in pieces:
        heights = jnp.exp(jax.random.uniform(jax.random.fold_in(own, axis_at), (parts,), jnp.float32, smallest / len(pieces), top_value / len(pieces)))
        factor_of = factor_of * jnp.repeat(heights, dims[axis_at] // parts).reshape([-1 if axis == axis_at else 1 for axis in range(len(dims))])
    return factor_of


def normal_values(stream_key, shape, deviation, bound, cuts=(), kind=jnp.bfloat16):
    level = steps_of(stream_key, shape, cuts, -0.22, 0.18) if cuts else 1.0
    entries = jax.random.normal(stream_key, shape, jnp.float32) * deviation * level
    return jnp.minimum(jnp.maximum(entries, -bound), bound).astype(kind)


def setup_inputs(seed: int = 0, part: int = 0) -> dict:
    splits = jax.random.split(jax.random.key(seed), 11)
    part_splits = jax.random.split(jax.random.fold_in(splits[10], part), 11)
    return {
        "hidden_in": draw_hidden_in(jax.random.fold_in(jax.random.fold_in(splits[10], part), 71), part),
        "norm_gain": jnp.clip(1.0 + 0.18 * jax.random.normal(splits[1], (1, MODEL_DIM), jnp.float32), 0.099609375, 1.8984375).astype(jnp.bfloat16),
        "w_query": draw_w_query(jax.random.fold_in(splits[10], 71), part),
        "w_key": draw_w_key(jax.random.fold_in(splits[10], 71), part),
        "w_value": normal_values(splits[4], (MODEL_DIM, KVHEADS * HEAD_DIM), MODEL_DIM ** -0.5, 0.0625, ((1, 16),)),
        "w_out": normal_values(splits[5], (QHEADS * HEAD_DIM, MODEL_DIM), (QHEADS * HEAD_DIM) ** -0.5, 0.09375, ((1, 16),)),
        "cache_keys": draw_cache_keys(jax.random.fold_in(jax.random.fold_in(splits[10], part), 71), part),
        "cache_values": normal_values(part_splits[7], (CONTEXT, KVHEADS, HEAD_DIM), 1.0, 6.0, ((0, 16),)),
        "offset": jax.random.randint(part_splits[8], (1,), CONTEXT - CACHE_DEV // 2, CONTEXT + 1).astype(jnp.int32),
        "length": jax.random.randint(part_splits[9], (1,), CONTEXT, CONTEXT + NEW_TOKENS + 1).astype(jnp.int32),
    }


EPSILON = 1e-05
ROPE_BASE = 500000.0
NEG_FILL = -1e+30

def rotate(vectors, positions):
    half_dim = vectors.shape[-1] // 2
    inverse = ROPE_BASE ** (-(jnp.arange(half_dim, dtype=jnp.float32) * 2.0 / vectors.shape[-1]))
    angles = positions.astype(jnp.float32)[:, None] * inverse[None, :]
    cosine = jnp.cos(angles)[:, None, :]
    sine_val = jnp.sin(angles)[:, None, :]
    first = vectors[..., :half_dim]
    second = vectors[..., half_dim:]
    return jnp.concatenate([first * cosine - second * sine_val, second * cosine + first * sine_val], axis=-1)

def reference(hidden_in, norm_gain, w_query, w_key, w_value, w_out, cache_keys, cache_values, offset, length):
    values_f = hidden_in.astype(jnp.float32)
    normed = (values_f * lax.rsqrt(lax.optimization_barrier(jnp.mean(values_f * values_f, axis=1, keepdims=True)) + EPSILON) * norm_gain.astype(jnp.float32)).astype(jnp.bfloat16)
    queries = jnp.dot(normed, w_query, preferred_element_type=jnp.float32).astype(jnp.bfloat16)
    fresh_keys = jnp.dot(normed, w_key, preferred_element_type=jnp.float32).astype(jnp.bfloat16)
    fresh_values = jnp.dot(normed, w_value, preferred_element_type=jnp.float32).astype(jnp.bfloat16)
    start = offset[0]
    positions = start + jnp.arange(NEW_TOKENS, dtype=jnp.int32)
    queries_rot = rotate(queries.astype(jnp.float32).reshape(NEW_TOKENS, QHEADS, HEAD_DIM), positions).astype(jnp.bfloat16)
    keys_rot = rotate(fresh_keys.astype(jnp.float32).reshape(NEW_TOKENS, KVHEADS, HEAD_DIM), positions).astype(jnp.bfloat16)
    key_rows = jnp.concatenate([cache_keys, keys_rot], axis=0).astype(jnp.float32)
    value_rows = jnp.concatenate([cache_values, fresh_values.reshape(NEW_TOKENS, KVHEADS, HEAD_DIM)], axis=0).astype(jnp.float32)
    key_index = jnp.arange(CONTEXT + NEW_TOKENS, dtype=jnp.int32)
    fresh_index = key_index - CONTEXT
    in_prefix = key_index < CONTEXT
    prefix_ok = key_index < start
    fresh_ok = start + fresh_index < length[0]
    group_size = QHEADS // KVHEADS
    score_scale = 1.0 / math.sqrt(HEAD_DIM)
    block_rows = 16

    def attend(block_start):
        query_block = lax.dynamic_slice_in_dim(queries_rot, block_start, block_rows, 0).astype(jnp.float32)
        query_pos = block_start + jnp.arange(block_rows, dtype=jnp.int32)
        allowed = jnp.where(in_prefix[None, :], prefix_ok[None, :], (fresh_index[None, :] <= query_pos[:, None]) & fresh_ok[None, :])
        outputs = []
        for group in range(KVHEADS):
            grouped = query_block[:, group * group_size:(group + 1) * group_size, :]
            scores = jnp.einsum('tgd,kd->tgk', grouped, key_rows[:, group, :]) * score_scale
            scores = jnp.where(allowed[:, None, :], scores, NEG_FILL)
            peak = lax.optimization_barrier(jnp.max(scores, axis=-1, keepdims=True))
            weights = jnp.exp(scores - peak)
            total = lax.optimization_barrier(jnp.sum(weights, axis=-1))
            rounded = lax.optimization_barrier(weights.astype(jnp.bfloat16)).astype(jnp.float32)
            mixed = jnp.einsum('tgk,kd->tgd', rounded, value_rows[:, group, :])
            outputs.append(mixed / total[..., None])
        return jnp.concatenate(outputs, axis=1)
    starts = jnp.arange(0, NEW_TOKENS, block_rows, dtype=jnp.int32)
    blocks = lax.map(attend, starts)
    attention = blocks.reshape(NEW_TOKENS, QHEADS * HEAD_DIM).astype(jnp.bfloat16)
    return jnp.dot(attention, w_out, preferred_element_type=jnp.float32).astype(jnp.bfloat16)
```

```python
import functools
import math

import jax
import jax.numpy as jnp
from jax import lax
from jax.experimental import pallas as pl
from jax.experimental.pallas import tpu as pltpu
from jax.sharding import PartitionSpec as P

QHEADS = 32
KVHEADS = 4
HEAD_DIM = 128


EPSILON = 1e-05
ROPE_BASE = 500000.0
NEG_FILL = -1e30


def rotate(vectors, positions):
    half_dim = vectors.shape[-1] // 2
    inverse = ROPE_BASE ** (-(jnp.arange(half_dim, dtype=jnp.float32) * 2.0 / vectors.shape[-1]))
    angles = positions.astype(jnp.float32)[:, None] * inverse[None, :]
    cosine = jnp.cos(angles)[:, None, :]
    sine_val = jnp.sin(angles)[:, None, :]
    first = vectors[..., :half_dim]
    second = vectors[..., half_dim:]
    return jnp.concatenate(
        [first * cosine - second * sine_val, second * cosine + first * sine_val], axis=-1
    )


def general_body(
    hidden_in, norm_gain, w_query, w_key, w_value, w_out, cache_keys, cache_values, offset, length
):
    my_index = lax.axis_index("weight")
    new_rows = hidden_in.shape[0]
    gathered, gain_all = (
        lax.all_gather(hidden_in, "weight", axis=1, tiled=True),
        lax.all_gather(norm_gain, "weight", axis=1, tiled=True),
    )
    values_f = gathered.astype(jnp.float32)
    normed = (
        values_f
        * lax.rsqrt(jnp.mean(values_f * values_f, axis=1, keepdims=True) + EPSILON)
        * gain_all.astype(jnp.float32)
    ).astype(jnp.bfloat16)
    query_cols = jnp.dot(normed, w_query, preferred_element_type=jnp.float32).astype(jnp.bfloat16)
    key_cols = jnp.dot(normed, w_key, preferred_element_type=jnp.float32).astype(jnp.bfloat16)
    value_cols = jnp.dot(normed, w_value, preferred_element_type=jnp.float32).astype(jnp.bfloat16)
    queries = lax.all_gather(query_cols, "weight", axis=1, tiled=True)
    fresh = lax.all_to_all(
        jnp.stack([key_cols, value_cols]), "weight", split_axis=1, concat_axis=2, tiled=True
    )
    own_rows = fresh.shape[1]
    start = offset[0]
    query_pos = start + jnp.arange(new_rows, dtype=jnp.int32)
    queries_rot = rotate(
        queries.astype(jnp.float32).reshape(new_rows, QHEADS, HEAD_DIM), query_pos
    ).astype(jnp.bfloat16)
    fresh_index = my_index * own_rows + jnp.arange(own_rows, dtype=jnp.int32)
    keys_rot = rotate(
        fresh[0].astype(jnp.float32).reshape(own_rows, KVHEADS, HEAD_DIM), start + fresh_index
    ).astype(jnp.bfloat16)
    fresh_values = fresh[1].reshape(own_rows, KVHEADS, HEAD_DIM)
    cache_rows = cache_keys.shape[0]
    prefix_ok = my_index * cache_rows + jnp.arange(cache_rows, dtype=jnp.int32) < start
    fresh_ok = (fresh_index[None, :] <= jnp.arange(new_rows, dtype=jnp.int32)[:, None]) & (
        start + fresh_index < length[0]
    )[None, :]
    group_size = QHEADS // KVHEADS
    score_scale = 1.0 / math.sqrt(HEAD_DIM)
    peaks = []
    totals = []
    mixes = []
    for group in range(KVHEADS):
        grouped = queries_rot[:, group * group_size : (group + 1) * group_size, :]
        prefix_scores = (
            jnp.einsum(
                "tgd,kd->tgk", grouped, cache_keys[:, group, :], preferred_element_type=jnp.float32
            )
            * score_scale
        )
        prefix_scores = jnp.where(prefix_ok[None, None, :], prefix_scores, NEG_FILL)
        fresh_scores = (
            jnp.einsum(
                "tgd,kd->tgk", grouped, keys_rot[:, group, :], preferred_element_type=jnp.float32
            )
            * score_scale
        )
        fresh_scores = jnp.where(fresh_ok[:, None, :], fresh_scores, NEG_FILL)
        peak = jnp.maximum(jnp.max(prefix_scores, axis=-1), jnp.max(fresh_scores, axis=-1))
        prefix_weights = jnp.exp(prefix_scores - peak[..., None])
        fresh_weights = jnp.exp(fresh_scores - peak[..., None])
        total = jnp.sum(prefix_weights, axis=-1) + jnp.sum(fresh_weights, axis=-1)
        mixed = jnp.einsum(
            "tgk,kd->tgd",
            prefix_weights.astype(jnp.bfloat16),
            cache_values[:, group, :],
            preferred_element_type=jnp.float32,
        )
        mixed = mixed + jnp.einsum(
            "tgk,kd->tgd",
            fresh_weights.astype(jnp.bfloat16),
            fresh_values[:, group, :],
            preferred_element_type=jnp.float32,
        )
        peaks.append(peak)
        totals.append(total)
        mixes.append(mixed)
    local_peak = jnp.concatenate(peaks, axis=1)
    local_total = jnp.concatenate(totals, axis=1)
    local_mixed = jnp.concatenate(mixes, axis=1)
    global_peak = lax.pmax(local_peak.astype(jnp.bfloat16), "weight").astype(local_peak.dtype)
    factor = jnp.exp(local_peak - global_peak)
    scaled_mixed = (local_mixed * factor[..., None]).reshape(new_rows, QHEADS * HEAD_DIM)
    mixed_share = lax.psum_scatter(scaled_mixed, "weight", scatter_dimension=1, tiled=True)
    denominator = lax.psum(local_total * factor, "weight")
    share_cols = mixed_share.shape[1]
    head_of = (my_index * share_cols + jnp.arange(share_cols, dtype=jnp.int32)) // HEAD_DIM
    selector = (head_of[:, None] == jnp.arange(QHEADS, dtype=jnp.int32)[None, :]).astype(
        jnp.float32
    )
    denom_share = jnp.dot(denominator, selector.T, precision=lax.Precision.HIGHEST)
    attention_share = (mixed_share / denom_share).astype(jnp.bfloat16)
    attention = lax.all_gather(attention_share, "weight", axis=1, tiled=True)
    return jnp.dot(attention, w_out, preferred_element_type=jnp.float32).astype(jnp.bfloat16)


PLANES = 4
PLANE = 4
PAD_ROWS = 16
FUSED_DEVICES = PLANES * PLANE


def near_order(z):
    half = lax.div(z, 2)
    return [z, z + 1 - 2 * lax.rem(z, 2), 2 - half, 3 * (1 - half)]


def fused_kernel(
    start_ref, length_ref, hidden, w_query, wk_t, wv_t, w_out, kv, cos_ref, sin_ref,
    out_ref,
    xg, wq, wkv, wo, kvb, pq, acc, peak, total, so, sl, ro, rl, at, rinv, qacc, kacc, oacc,
    ss1, rs1, sskv, rskv, ss2, rs2, ss3, rs3, ss4, rs4, local_sem,
):
    me = lax.axis_index("weight")
    z = lax.div(me, 4)
    y = lax.rem(lax.div(me, 2), 2)
    c = lax.rem(me, 2)
    q = lax.rem(me, 4)
    plane0 = z * 4
    up, down = me + 4, me - 4
    yn = me + 2 - 4 * y
    sib = me + 1 - 2 * c
    ynsib = yn + 1 - 2 * c
    order = near_order(z)
    tokens = out_ref.shape[0]
    depth = xg.shape[2]
    keys = kvb.shape[2]

    def remote(src, dst, ssem, rsem, dev):
        return pltpu.make_async_remote_copy(
            src_ref=src, dst_ref=dst, send_sem=ssem, recv_sem=rsem,
            device_id={"weight": dev}, device_id_type=pl.DeviceIdType.MESH,
        )

    barrier = pltpu.get_barrier_semaphore()
    for k in range(1, 4):
        for dev in (order[k] * 4 + q, plane0 + lax.rem(q + k, 4)):
            pl.semaphore_signal(
                barrier, inc=1, device_id={"weight": dev}, device_id_type=pl.DeviceIdType.MESH
            )
    pl.semaphore_wait(barrier, 6)

    def gather(slots, own, ss, rs, consume, between):
        def cp(i, src, d, dev):
            return remote(src, slots.at[i], ss.at[i, d], rs.at[i], dev)

        def fan(i, src, go_up, go_down):
            if go_up is not None:
                @pl.when(go_up)
                def _():
                    cp(i, src, 0, up).start()
            if go_down is not None:
                @pl.when(go_down)
                def _():
                    cp(i, src, 1, down).start()
            cp(i, src, 2, yn).start()
            cp(i, src, 3, sib).start()

        fan(me, own, z < 3, z > 0)
        between(-1)
        for k in range(4):
            if k < 3:
                o = order[k + 1]
                i = o * 4 + q
                cp(i, slots.at[i], 2, yn).wait_recv()
                fan(i, slots.at[i], (o < z) & (z < 3), (o > z) & (z > 0))
            i = order[k] * 4 + lax.rem(yn, 4)
            cp(i, slots.at[i], 2, yn).wait_recv()
            cp(i, slots.at[i], 3, sib).start()
            between(k)
            consume(order[k] * 4 + q, slots)
            consume(order[k] * 4 + lax.rem(yn, 4), slots)
            for other in (sib, ynsib):
                i = order[k] * 4 + lax.rem(other, 4)
                cp(i, slots.at[i], 3, sib).wait_recv()
                consume(i, slots)

        def finish():
            @pl.when(z < 3)
            def _():
                cp(me, own, 0, up).wait_send()
            @pl.when(z > 0)
            def _():
                cp(me, own, 1, down).wait_send()
            cp(me, own, 2, yn).wait_send()
            cp(me, own, 3, sib).wait_send()
            for k in range(1, 4):
                o = order[k]
                i = o * 4 + q
                @pl.when((o < z) & (z < 3))
                def _():
                    cp(i, slots.at[i], 0, up).wait_send()
                @pl.when((o > z) & (z > 0))
                def _():
                    cp(i, slots.at[i], 1, down).wait_send()
                cp(i, slots.at[i], 2, yn).wait_send()
                cp(i, slots.at[i], 3, sib).wait_send()
            for k in range(4):
                i = order[k] * 4 + lax.rem(yn, 4)
                cp(i, slots.at[i], 3, sib).wait_send()

        return finish

    own_copy = pltpu.make_async_copy(hidden, xg.at[me], local_sem.at[0])
    loads = [
        pltpu.make_async_copy(w_query, wq, local_sem.at[1]),
        pltpu.make_async_copy(wk_t, wkv.at[pl.ds(0, 32)], local_sem.at[2]),
        pltpu.make_async_copy(wv_t, wkv.at[pl.ds(32, 32)], local_sem.at[3]),
        pltpu.make_async_copy(kv.at[z], kvb.at[z], local_sem.at[4]),
        pltpu.make_async_copy(w_out, wo, local_sem.at[5]),
    ]

    def kv_copy(k):
        return remote(kv.at[order[k]], kvb.at[z], sskv.at[order[k]], rskv.at[z], order[k] * 4 + q)

    def kv_arrival(k):
        o = order[k]
        return remote(kv.at[o], kvb.at[o], sskv.at[o], rskv.at[o], o * 4 + q)

    def between_first(k):
        if k == -1:
            own_copy.start()
            for load in loads:
                load.start()
            rinv[...] = jnp.zeros_like(rinv)
            own_copy.wait()
        if k == KV_AFTER:
            for j in range(1, 4):
                kv_copy(j).start()

    def squares(i, slots):
        x = slots[i, 0:tokens, :].astype(jnp.float32)
        xx = x * x
        part = xx[:, 0:128]
        for j in range(1, depth // 128):
            part = part + xx[:, j * 128 : (j + 1) * 128]
        rinv[...] += part

    finish_first = gather(xg, hidden, ss1, rs1, squares, between_first)

    mean = jnp.sum(rinv[...], axis=1, keepdims=True) * (1.0 / (depth * FUSED_DEVICES))
    rinv[...] = jnp.broadcast_to(lax.rsqrt(mean + EPSILON), rinv.shape)
    for load in loads[:3]:
        load.wait()
    qacc[...] = jnp.zeros_like(qacc)
    kacc[...] = jnp.zeros_like(kacc)

    def project(i, carry):
        x = xg[i, 0:tokens, :].astype(jnp.float32)
        gain = xg[i, tokens : tokens + 1, :].astype(jnp.float32)
        scale = jnp.concatenate([rinv[...]] * (depth // 128), axis=1)
        normed = (x * scale * gain).astype(jnp.bfloat16)
        first = pl.multiple_of(i * depth, depth)
        qacc[...] += jnp.dot(normed, wq[pl.ds(first, depth), :], preferred_element_type=jnp.float32)
        kacc[...] += lax.dot_general(
            normed, wkv[:, pl.ds(first, depth)], (((1,), (1,)), ((), ())),
            preferred_element_type=jnp.float32,
        )
        return carry

    lax.fori_loop(0, FUSED_DEVICES, project, 0)

    def turn(x, cosine, sine):
        return (x * cosine + pltpu.roll(x, 64, 1) * sine).astype(jnp.bfloat16)

    queries = qacc[...].astype(jnp.bfloat16).astype(jnp.float32)
    for h in range(2):
        at_cols = slice(h * HEAD_DIM, (h + 1) * HEAD_DIM)
        pq[q, :, at_cols] = turn(queries[:, at_cols], cos_ref[...], sin_ref[...])
    pq[q, :, 256:320] = kacc[...].astype(jnp.bfloat16)
    pq[q, :, 320:384] = jnp.zeros((tokens, 64), jnp.bfloat16)

    def pcp(i, d, dev):
        return remote(pq.at[i], pq.at[i], ss2.at[i, d], rs2.at[i], dev)

    yq, sq, ysq = lax.rem(yn, 4), lax.rem(sib, 4), lax.rem(ynsib, 4)
    pcp(q, 0, yn).start()
    pcp(q, 1, sib).start()

    def clear(h, carry):
        acc[h] = jnp.zeros(acc.shape[1:], jnp.float32)
        peak[h] = jnp.full(peak.shape[1:], NEG_FILL, jnp.float32)
        total[h] = jnp.zeros(total.shape[1:], jnp.float32)
        return carry

    lax.fori_loop(0, 8, clear, 0)
    pcp(yq, 0, yn).wait_recv()
    pcp(yq, 1, sib).start()
    pcp(sq, 1, sib).wait_recv()
    pcp(ysq, 1, sib).wait_recv()

    start = start_ref[0]
    length = length_ref[0]
    score_scale = 1.0 / math.sqrt(HEAD_DIM)

    def attend(p, key_rows, value_rows, allowed):
        for h in range(2):
            n = p * 2 + h
            scores = lax.dot_general(
                key_rows, pq[p, :, h * HEAD_DIM : (h + 1) * HEAD_DIM], (((1,), (1,)), ((), ())),
                preferred_element_type=jnp.float32,
            ) * score_scale
            scores = jnp.where(allowed, scores, NEG_FILL)
            old = peak[n]
            new = jnp.maximum(old, jnp.max(scores, axis=0, keepdims=True))
            weights = jnp.exp(scores - new)
            factor = jnp.exp(old - new)
            peak[n] = new
            total[n] = total[n] * factor + jnp.sum(weights, axis=0, keepdims=True)
            acc[n] = acc[n] * factor + lax.dot_general(
                value_rows, weights.astype(jnp.bfloat16), (((0,), (0,)), ((), ())),
                preferred_element_type=jnp.float32,
            )

    loads[3].wait()
    for k in range(4):
        o = order[k]
        if k > 0:
            kv_arrival(k).wait_recv()

        def one(p, carry):
            row = lax.broadcasted_iota(jnp.int32, (keys, tokens), 0)
            allowed = row < start - (o * 4 + q) * keys
            attend(p, kvb[o, 0], kvb[o, 1], allowed)
            return carry

        lax.fori_loop(0, PLANE, one, 0)

    own_rows = tokens // PLANE
    row0 = pl.multiple_of(q * own_rows, own_rows)
    fresh_key = jnp.concatenate(
        [pq[p, pl.ds(row0, own_rows), 256:288] for p in range(PLANE)], axis=1
    ).astype(jnp.float32)
    fresh_key = turn(fresh_key, cos_ref[pl.ds(row0, own_rows), :], sin_ref[pl.ds(row0, own_rows), :])
    fresh_value = jnp.concatenate(
        [pq[p, pl.ds(row0, own_rows), 288:320] for p in range(PLANE)], axis=1
    )

    def one_fresh(p, carry):
        row = row0 + lax.broadcasted_iota(jnp.int32, (own_rows, tokens), 0)
        token = lax.broadcasted_iota(jnp.int32, (own_rows, tokens), 1)
        attend(p, fresh_key, fresh_value, (row <= token) & (row < length - start))
        return carry

    lax.fori_loop(0, PLANE, one_fresh, 0)

    def pack(p, carry):
        for h in range(2):
            n = p * 2 + h
            so[p, h * HEAD_DIM : (h + 1) * HEAD_DIM, :] = (acc[n] / total[n]).astype(jnp.bfloat16)
            sl[p, h : h + 1, :] = peak[n] + jnp.log(total[n])
        sl[p, 2:8, :] = jnp.zeros((6, tokens), jnp.float32)
        return carry

    lax.fori_loop(0, PLANE, pack, 0)
    sends = []
    for j in (2, 3, 1):
        p = lax.rem(q + j, 4)
        sends.append(remote(so.at[p], ro.at[q], ss3.at[j, 0], rs3.at[j, 0], plane0 + p))
        sends.append(remote(sl.at[p], rl.at[q], ss3.at[j, 1], rs3.at[j, 1], plane0 + p))
    for send in sends:
        send.start()
    oacc[...] = jnp.zeros_like(oacc)
    loads[4].wait()
    for j in (1, 2, 3):
        p = lax.rem(q + 4 - j, 4)
        remote(so.at[p], ro.at[p], ss3.at[j, 0], rs3.at[j, 0], plane0 + p).wait_recv()
        remote(sl.at[p], rl.at[p], ss3.at[j, 1], rs3.at[j, 1], plane0 + p).wait_recv()
    froms = [lax.rem(q + j, 4) for j in (1, 2, 3)]
    for h in range(2):
        lses = [sl[q, h : h + 1, :]] + [rl[p, h : h + 1, :] for p in froms]
        rows = slice(h * HEAD_DIM, (h + 1) * HEAD_DIM)
        parts = [so[q, rows, :]] + [ro[p, rows, :] for p in froms]
        top = jnp.maximum(jnp.maximum(lses[0], lses[1]), jnp.maximum(lses[2], lses[3]))
        shares = [jnp.exp(lse - top) for lse in lses]
        whole = shares[0] + shares[1] + shares[2] + shares[3]
        mixed = sum(part.astype(jnp.float32) * share for part, share in zip(parts, shares)) / whole
        at[me, :, rows] = jnp.transpose(mixed).astype(jnp.bfloat16)

    def project_out(i, slots):
        width = slots.shape[2]
        first = pl.multiple_of(i * width, width)
        oacc[...] += jnp.dot(slots[i], wo[pl.ds(first, width), :], preferred_element_type=jnp.float32)

    finish_second = gather(at, at.at[me], ss4, rs4, project_out, lambda k: None)
    out_ref[...] = oacc[...].astype(jnp.bfloat16)
    finish_first()
    finish_second()
    for k in range(1, 4):
        kv_copy(k).wait_send()
    pcp(q, 0, yn).wait_send()
    pcp(q, 1, sib).wait_send()
    pcp(yq, 1, sib).wait_send()
    for send in sends:
        send.wait_send()


KV_AFTER = 1


def fused_body(
    hidden_in, norm_gain, w_query, w_key, w_value, w_out, cache_keys, cache_values, offset, length
):
    tokens, depth = hidden_in.shape
    keys = cache_keys.shape[0]
    hidden = jnp.concatenate([hidden_in, jnp.broadcast_to(norm_gain, (PAD_ROWS, depth))], axis=0)
    kv = jnp.transpose(jnp.stack([cache_keys, cache_values]), (2, 0, 1, 3))
    half_dim = HEAD_DIM // 2
    inverse = ROPE_BASE ** (-(jnp.arange(half_dim, dtype=jnp.float32) * 2.0 / HEAD_DIM))
    positions = offset[0] + jnp.arange(tokens, dtype=jnp.int32)
    angles = positions.astype(jnp.float32)[:, None] * inverse[None, :]
    cosine, sine = jnp.cos(angles), jnp.sin(angles)
    cosine = jnp.concatenate([cosine, cosine], axis=1)
    sine = jnp.concatenate([-sine, sine], axis=1)
    smem = pl.BlockSpec(memory_space=pltpu.SMEM)
    vmem = pl.BlockSpec(memory_space=pltpu.VMEM)
    hbm = pl.BlockSpec(memory_space=pl.ANY)
    bf16, f32 = jnp.bfloat16, jnp.float32
    dma = pltpu.SemaphoreType.DMA
    n = FUSED_DEVICES
    return pl.pallas_call(
        fused_kernel,
        out_shape=jax.ShapeDtypeStruct((tokens, w_out.shape[1]), bf16),
        in_specs=[smem, smem, hbm, hbm, hbm, hbm, hbm, hbm, vmem, vmem],
        out_specs=vmem,
        scratch_shapes=[
            pltpu.VMEM((n, tokens + PAD_ROWS, depth), bf16),
            pltpu.VMEM(w_query.shape, bf16),
            pltpu.VMEM((64, w_query.shape[0]), bf16),
            pltpu.VMEM(w_out.shape, bf16),
            pltpu.VMEM((PLANES, 2, keys, HEAD_DIM), bf16),
            pltpu.VMEM((PLANE, tokens, 384), bf16),
            pltpu.VMEM((8, HEAD_DIM, tokens), f32),
            pltpu.VMEM((8, 1, tokens), f32),
            pltpu.VMEM((8, 1, tokens), f32),
            pltpu.VMEM((PLANE, 2 * HEAD_DIM, tokens), bf16),
            pltpu.VMEM((PLANE, 8, tokens), f32),
            pltpu.VMEM((PLANE, 2 * HEAD_DIM, tokens), bf16),
            pltpu.VMEM((PLANE, 8, tokens), f32),
            pltpu.VMEM((n, tokens, 2 * HEAD_DIM), bf16),
            pltpu.VMEM((tokens, 128), f32),
            pltpu.VMEM((tokens, 2 * HEAD_DIM), f32),
            pltpu.VMEM((tokens, 64), f32),
            pltpu.VMEM((tokens, w_out.shape[1]), f32),
            dma((n, 4)), dma((n,)),
            dma((PLANES,)), dma((PLANES,)),
            dma((PLANE, 2)), dma((PLANE,)),
            dma((4, 2)), dma((4, 2)),
            dma((n, 4)), dma((n,)),
            dma((6,)),
        ],
        compiler_params=pltpu.CompilerParams(
            collective_id=0, has_side_effects=True, vmem_limit_bytes=50 * 1024 * 1024
        ),
        cost_estimate=pl.CostEstimate(flops=6_000_000_000, bytes_accessed=16_000_000, transcendentals=6_000_000),
    )(offset, length, hidden, w_query, w_key.T, w_value.T, w_out, kv, cosine, sine)


def solution(mesh):
    body = fused_body if mesh.shape["weight"] == FUSED_DEVICES else general_body
    return jax.shard_map(
        body,
        mesh=mesh,
        in_specs=(
            P("groups", "weight"),
            P(None, "weight"),
            P(None, "weight"),
            P(None, "weight"),
            P(None, "weight"),
            P(None, "weight"),
            P(("groups", "weight"), None, None),
            P(("groups", "weight"), None, None),
            P("groups"),
            P("groups"),
        ),
        out_specs=P("groups", "weight"),
        check_vma=False,
    )
```

```python
import functools
import math

import jax
import jax.numpy as jnp
from jax import lax
from jax.experimental import pallas as pl
from jax.experimental.pallas import tpu as pltpu
from jax.sharding import PartitionSpec as P

QHEADS = 32
KVHEADS = 4
HEAD_DIM = 128


EPSILON = 1e-05
ROPE_BASE = 500000.0
NEG_FILL = -1e30


def rotate(vectors, positions):
    half_dim = vectors.shape[-1] // 2
    inverse = ROPE_BASE ** (-(jnp.arange(half_dim, dtype=jnp.float32) * 2.0 / vectors.shape[-1]))
    angles = positions.astype(jnp.float32)[:, None] * inverse[None, :]
    cosine = jnp.cos(angles)[:, None, :]
    sine_val = jnp.sin(angles)[:, None, :]
    first = vectors[..., :half_dim]
    second = vectors[..., half_dim:]
    return jnp.concatenate(
        [first * cosine - second * sine_val, second * cosine + first * sine_val], axis=-1
    )


def general_body(
    hidden_in, norm_gain, w_query, w_key, w_value, w_out, cache_keys, cache_values, offset, length
):
    my_index = lax.axis_index("weight")
    new_rows = hidden_in.shape[0]
    gathered, gain_all = (
        lax.all_gather(hidden_in, "weight", axis=1, tiled=True),
        lax.all_gather(norm_gain, "weight", axis=1, tiled=True),
    )
    values_f = gathered.astype(jnp.float32)
    normed = (
        values_f
        * lax.rsqrt(jnp.mean(values_f * values_f, axis=1, keepdims=True) + EPSILON)
        * gain_all.astype(jnp.float32)
    ).astype(jnp.bfloat16)
    query_cols = jnp.dot(normed, w_query, preferred_element_type=jnp.float32).astype(jnp.bfloat16)
    key_cols = jnp.dot(normed, w_key, preferred_element_type=jnp.float32).astype(jnp.bfloat16)
    value_cols = jnp.dot(normed, w_value, preferred_element_type=jnp.float32).astype(jnp.bfloat16)
    queries = lax.all_gather(query_cols, "weight", axis=1, tiled=True)
    fresh = lax.all_to_all(
        jnp.stack([key_cols, value_cols]), "weight", split_axis=1, concat_axis=2, tiled=True
    )
    own_rows = fresh.shape[1]
    start = offset[0]
    query_pos = start + jnp.arange(new_rows, dtype=jnp.int32)
    queries_rot = rotate(
        queries.astype(jnp.float32).reshape(new_rows, QHEADS, HEAD_DIM), query_pos
    ).astype(jnp.bfloat16)
    fresh_index = my_index * own_rows + jnp.arange(own_rows, dtype=jnp.int32)
    keys_rot = rotate(
        fresh[0].astype(jnp.float32).reshape(own_rows, KVHEADS, HEAD_DIM), start + fresh_index
    ).astype(jnp.bfloat16)
    fresh_values = fresh[1].reshape(own_rows, KVHEADS, HEAD_DIM)
    cache_rows = cache_keys.shape[0]
    prefix_ok = my_index * cache_rows + jnp.arange(cache_rows, dtype=jnp.int32) < start
    fresh_ok = (fresh_index[None, :] <= jnp.arange(new_rows, dtype=jnp.int32)[:, None]) & (
        start + fresh_index < length[0]
    )[None, :]
    group_size = QHEADS // KVHEADS
    score_scale = 1.0 / math.sqrt(HEAD_DIM)
    peaks = []
    totals = []
    mixes = []
    for group in range(KVHEADS):
        grouped = queries_rot[:, group * group_size : (group + 1) * group_size, :]
        prefix_scores = (
            jnp.einsum(
                "tgd,kd->tgk", grouped, cache_keys[:, group, :], preferred_element_type=jnp.float32
            )
            * score_scale
        )
        prefix_scores = jnp.where(prefix_ok[None, None, :], prefix_scores, NEG_FILL)
        fresh_scores = (
            jnp.einsum(
                "tgd,kd->tgk", grouped, keys_rot[:, group, :], preferred_element_type=jnp.float32
            )
            * score_scale
        )
        fresh_scores = jnp.where(fresh_ok[:, None, :], fresh_scores, NEG_FILL)
        peak = jnp.maximum(jnp.max(prefix_scores, axis=-1), jnp.max(fresh_scores, axis=-1))
        prefix_weights = jnp.exp(prefix_scores - peak[..., None])
        fresh_weights = jnp.exp(fresh_scores - peak[..., None])
        total = jnp.sum(prefix_weights, axis=-1) + jnp.sum(fresh_weights, axis=-1)
        mixed = jnp.einsum(
            "tgk,kd->tgd",
            prefix_weights.astype(jnp.bfloat16),
            cache_values[:, group, :],
            preferred_element_type=jnp.float32,
        )
        mixed = mixed + jnp.einsum(
            "tgk,kd->tgd",
            fresh_weights.astype(jnp.bfloat16),
            fresh_values[:, group, :],
            preferred_element_type=jnp.float32,
        )
        peaks.append(peak)
        totals.append(total)
        mixes.append(mixed)
    local_peak = jnp.concatenate(peaks, axis=1)
    local_total = jnp.concatenate(totals, axis=1)
    local_mixed = jnp.concatenate(mixes, axis=1)
    global_peak = lax.pmax(local_peak.astype(jnp.bfloat16), "weight").astype(local_peak.dtype)
    factor = jnp.exp(local_peak - global_peak)
    scaled_mixed = (local_mixed * factor[..., None]).reshape(new_rows, QHEADS * HEAD_DIM)
    mixed_share = lax.psum_scatter(scaled_mixed, "weight", scatter_dimension=1, tiled=True)
    denominator = lax.psum(local_total * factor, "weight")
    share_cols = mixed_share.shape[1]
    head_of = (my_index * share_cols + jnp.arange(share_cols, dtype=jnp.int32)) // HEAD_DIM
    selector = (head_of[:, None] == jnp.arange(QHEADS, dtype=jnp.int32)[None, :]).astype(
        jnp.float32
    )
    denom_share = jnp.dot(denominator, selector.T, precision=lax.Precision.HIGHEST)
    attention_share = (mixed_share / denom_share).astype(jnp.bfloat16)
    attention = lax.all_gather(attention_share, "weight", axis=1, tiled=True)
    return jnp.dot(attention, w_out, preferred_element_type=jnp.float32).astype(jnp.bfloat16)


PLANES = 4
PLANE = 4
PAD_ROWS = 16
FUSED_DEVICES = PLANES * PLANE


def near_order(z):
    half = lax.div(z, 2)
    return [z, z + 1 - 2 * lax.rem(z, 2), 2 - half, 3 * (1 - half)]


def fused_kernel(
    start_ref, length_ref, hidden, w_query, wk_t, wv_t, w_out, kv, cos_ref, sin_ref,
    out_ref,
    xg, wq, wkv, wo, kb, vb, vt, pq, acc, peak, total, so, sl, ro, rl, at, rinv, qacc, kacc, oacc,
    ss1, rs1, sskv, rskv, ss2, rs2, ss3, rs3, ss4, rs4, local_sem,
):
    me = lax.axis_index("weight")
    z = lax.div(me, 4)
    y = lax.rem(lax.div(me, 2), 2)
    c = lax.rem(me, 2)
    q = lax.rem(me, 4)
    plane0 = z * 4
    up, down = me + 4, me - 4
    yn = me + 2 - 4 * y
    sib = me + 1 - 2 * c
    ynsib = yn + 1 - 2 * c
    order = near_order(z)
    tokens = out_ref.shape[0]
    depth = xg.shape[2]
    keys = kb.shape[1]

    def remote(src, dst, ssem, rsem, dev):
        return pltpu.make_async_remote_copy(
            src_ref=src, dst_ref=dst, send_sem=ssem, recv_sem=rsem,
            device_id={"weight": dev}, device_id_type=pl.DeviceIdType.MESH,
        )

    barrier = pltpu.get_barrier_semaphore()
    for k in range(1, 4):
        for dev in (order[k] * 4 + q, plane0 + lax.rem(q + k, 4)):
            pl.semaphore_signal(
                barrier, inc=1, device_id={"weight": dev}, device_id_type=pl.DeviceIdType.MESH
            )
    pl.semaphore_wait(barrier, 6)

    def gather(slots, own, ss, rs, direct):
        def cp(i, src, d, dev):
            return remote(src, slots.at[i], ss.at[i, d], rs.at[i], dev)

        def along(i, src, first, act):
            if direct:
                if first:
                    for k in range(1, 4):
                        act(cp(i, src, 3 + k, order[k] * 4 + q))
                return
            o = lax.div(i, 4)

            @pl.when((o <= z) & (z < 3))
            def _():
                act(cp(i, src, 0, up))

            @pl.when((o >= z) & (z > 0))
            def _():
                act(cp(i, src, 1, down))

        def across(i, src, act):
            act(cp(i, src, 2, yn))
            act(cp(i, src, 3, sib))

        def begin():
            along(me, own, True, lambda copy: copy.start())
            across(me, own, lambda copy: copy.start())

        def forward(k):
            if k < 3:
                i = order[k + 1] * 4 + q
                cp(i, slots.at[i], 2, yn).wait_recv()
                along(i, slots.at[i], False, lambda copy: copy.start())
                across(i, slots.at[i], lambda copy: copy.start())
            i = order[k] * 4 + lax.rem(yn, 4)
            cp(i, slots.at[i], 2, yn).wait_recv()
            cp(i, slots.at[i], 3, sib).start()

        def consume(k, use):
            use(order[k] * 4 + q)
            use(order[k] * 4 + lax.rem(yn, 4))
            for other in (sib, ynsib):
                i = order[k] * 4 + lax.rem(other, 4)
                cp(i, slots.at[i], 3, sib).wait_recv()
                use(i)

        def finish():
            along(me, own, True, lambda copy: copy.wait_send())
            across(me, own, lambda copy: copy.wait_send())
            for k in range(1, 4):
                i = order[k] * 4 + q
                along(i, slots.at[i], False, lambda copy: copy.wait_send())
                across(i, slots.at[i], lambda copy: copy.wait_send())
            for k in range(4):
                i = order[k] * 4 + lax.rem(yn, 4)
                cp(i, slots.at[i], 3, sib).wait_send()

        return begin, forward, consume, finish

    own_copy = pltpu.make_async_copy(hidden, xg.at[me], local_sem.at[0])
    loads = [
        pltpu.make_async_copy(w_query, wq, local_sem.at[1]),
        pltpu.make_async_copy(wk_t, wkv.at[pl.ds(0, 32)], local_sem.at[2]),
        pltpu.make_async_copy(wv_t, wkv.at[pl.ds(32, 32)], local_sem.at[3]),
        pltpu.make_async_copy(kv.at[z, 0], kb.at[z], local_sem.at[4]),
        pltpu.make_async_copy(kv.at[z, 1], vb.at[z], local_sem.at[6]),
        pltpu.make_async_copy(w_out, wo, local_sem.at[5]),
    ]

    def kv_copies(k):
        o = order[k]
        return [
            remote(kv.at[o, j], buf.at[z], sskv.at[o, j], rskv.at[z, j], o * 4 + q)
            for j, buf in enumerate((kb, vb))
        ]

    def kv_arrivals(k):
        o = order[k]
        return [
            remote(kv.at[o, j], buf.at[o], sskv.at[o, j], rskv.at[o, j], o * 4 + q)
            for j, buf in enumerate((kb, vb))
        ]

    def between_first(k):
        if k == -1:
            own_copy.start()
            for load in loads:
                load.start()
            rinv[...] = jnp.zeros_like(rinv)
            own_copy.wait()
        if k == KV_AFTER:
            for j in range(1, 4):
                for copy in kv_copies(j):
                    copy.start()

    def squares(i):
        x = xg[i, 0:tokens, :].astype(jnp.float32)
        xx = x * x
        part = xx[:, 0:128]
        for j in range(1, depth // 128):
            part = part + xx[:, j * 128 : (j + 1) * 128]
        rinv[...] += part

    begin, forward, consume, finish_first = gather(xg, hidden, ss1, rs1, False)
    begin()
    between_first(-1)
    for k in range(4):
        forward(k)
        between_first(k)
        consume(k, squares)

    mean = jnp.sum(rinv[...], axis=1, keepdims=True) * (1.0 / (depth * FUSED_DEVICES))
    rinv[...] = jnp.broadcast_to(lax.rsqrt(mean + EPSILON), rinv.shape)
    for load in loads[:3]:
        load.wait()
    qacc[...] = jnp.zeros_like(qacc)
    kacc[...] = jnp.zeros_like(kacc)

    def project(i, carry):
        x = xg[i, 0:tokens, :].astype(jnp.float32)
        gain = xg[i, tokens : tokens + 1, :].astype(jnp.float32)
        scale = jnp.concatenate([rinv[...]] * (depth // 128), axis=1)
        normed = (x * scale * gain).astype(jnp.bfloat16)
        first = pl.multiple_of(i * depth, depth)
        qacc[...] += jnp.dot(normed, wq[pl.ds(first, depth), :], preferred_element_type=jnp.float32)
        kacc[...] += lax.dot_general(
            wkv[:, pl.ds(first, depth)], normed, (((1,), (1,)), ((), ())),
            preferred_element_type=jnp.float32,
        )
        return carry

    lax.fori_loop(0, FUSED_DEVICES, project, 0)

    def turn(x):
        return x * cos_ref[...] + pltpu.roll(x, 64, 1) * sin_ref[...]

    queries = qacc[...].astype(jnp.bfloat16).astype(jnp.float32)
    for h in range(2):
        rows = slice(h * HEAD_DIM, (h + 1) * HEAD_DIM)
        pq[q, rows, :] = jnp.transpose(turn(queries[:, rows])).astype(jnp.bfloat16)
    pq[q, 256:320, :] = kacc[...].astype(jnp.bfloat16)

    def pcp(i, d, dev):
        return remote(pq.at[i], pq.at[i], ss2.at[i, d], rs2.at[i], dev)

    yq, sq, ysq = lax.rem(yn, 4), lax.rem(sib, 4), lax.rem(ynsib, 4)
    near = [q, yq, ysq, sq]
    pcp(q, 0, yn).start()
    pcp(q, 1, sib).start()

    loads[3].wait()
    loads[4].wait()
    for k in range(1, 4):
        for copy in kv_arrivals(k):
            copy.wait_recv()
    for o in range(PLANES):
        vt[:, o * keys : (o + 1) * keys] = jnp.transpose(vb[o])

    start = start_ref[0]
    length = length_ref[0]
    score_scale = math.log2(math.e) / math.sqrt(HEAD_DIM)

    def attend(query, blocks):
        top = whole = mixed = None
        for key_rows, value_cols, allowed in blocks:
            scores = jnp.dot(key_rows, query, preferred_element_type=jnp.float32) * score_scale
            if allowed is not None:
                scores = jnp.where(allowed, scores, NEG_FILL)
            new = jnp.max(scores, axis=0, keepdims=True)
            if top is not None:
                new = jnp.maximum(top, new)
            weights = jnp.exp2(scores - new)
            part = jnp.sum(weights, axis=0, keepdims=True)
            product = jnp.dot(
                value_cols, weights.astype(jnp.bfloat16), preferred_element_type=jnp.float32
            )
            if top is not None:
                factor = jnp.exp2(top - new)
                part = part + whole * factor
                product = product + mixed * factor
            top, whole, mixed = new, part, product
        return top, whole, mixed

    def cache_blocks():
        row = lax.broadcasted_iota(jnp.int32, (keys, tokens), 0)
        last = row < start - ((PLANES - 1) * 4 + q) * keys
        return [
            (kb[o], vt[:, o * keys : (o + 1) * keys], last if o == PLANES - 1 else None)
            for o in range(PLANES)
        ]

    def head_rows(h):
        if isinstance(h, int):
            return pl.ds(h * HEAD_DIM, HEAD_DIM)
        return pl.ds(pl.multiple_of(h * HEAD_DIM, HEAD_DIM), HEAD_DIM)

    def keep(n, result):
        top, whole, mixed = result
        so[n] = (mixed * (1.0 / whole)).astype(jnp.bfloat16)
        sl[n, 0:1, :] = top + jnp.log2(whole)
        sl[n, 1:8, :] = jnp.zeros((7, tokens), jnp.float32)

    def mine(h, carry):
        peak[h], total[h], acc[h] = attend(pq[q, head_rows(h), :], cache_blocks())
        return carry

    lax.fori_loop(0, 2, mine, 0)

    pcp(yq, 0, yn).wait_recv()
    pcp(yq, 1, sib).start()
    pcp(sq, 1, sib).wait_recv()

    def part_copies(t, h, p, back):
        n = p * 2 + h
        m = q * 2 + h
        target = n if back else m
        return [
            remote(so.at[n], ro.at[target], ss3.at[t, h, 0], rs3.at[t, h, 0], plane0 + p),
            remote(sl.at[n], rl.at[target], ss3.at[t, h, 1], rs3.at[t, h, 1], plane0 + p),
        ]

    def theirs(t, h):
        p = near[t]
        keep(p * 2 + h, attend(pq[p, head_rows(h), :], cache_blocks()))
        for copy in part_copies(t, h, p, False):
            copy.start()

    theirs(1, 0)
    pcp(ysq, 1, sib).wait_recv()
    fresh_key = jnp.transpose(
        jnp.concatenate([pq[p, 256:288, :] for p in range(PLANE)], axis=0).astype(jnp.float32)
    )
    fresh_key = turn(fresh_key).astype(jnp.bfloat16)
    fresh_value = jnp.concatenate([pq[p, 288:320, :] for p in range(PLANE)], axis=0)
    row = lax.broadcasted_iota(jnp.int32, (tokens, tokens), 0)
    token = lax.broadcasted_iota(jnp.int32, (tokens, tokens), 1)
    fresh_ok = (row <= token) & (row < length - start)
    for h in range(2):
        top, whole, mixed = attend(
            pq[q, head_rows(h), :], [(fresh_key, fresh_value, fresh_ok)]
        )
        new = jnp.maximum(top, peak[h])
        one, two = jnp.exp2(top - new), jnp.exp2(peak[h] - new)
        keep(q * 2 + h, (new, whole * one + total[h] * two, mixed * one + acc[h] * two))
    theirs(2, 0)
    theirs(3, 0)

    gathers = [gather(at.at[h], at.at[h, me], ss4.at[h], rs4.at[h], True) for h in range(2)]

    def combine(h):
        for t in range(1, 4):
            for copy in part_copies(t, h, near[t], True):
                copy.wait_recv()
        lses = [sl[q * 2 + h, 0:1, :]] + [rl[near[t] * 2 + h, 0:1, :] for t in range(1, 4)]
        parts = [so[q * 2 + h]] + [ro[near[t] * 2 + h] for t in range(1, 4)]
        top = jnp.maximum(jnp.maximum(lses[0], lses[1]), jnp.maximum(lses[2], lses[3]))
        shares = [jnp.exp2(lse - top) for lse in lses]
        whole = shares[0] + shares[1] + shares[2] + shares[3]
        mixed = sum(part.astype(jnp.float32) * share for part, share in zip(parts, shares)) / whole
        at[h, me] = jnp.transpose(mixed).astype(jnp.bfloat16)
        gathers[h][0]()

    def project_out(h):
        def use(i):
            first = pl.multiple_of((i * 2 + h) * HEAD_DIM, HEAD_DIM)
            oacc[...] += jnp.dot(
                at[h, i], wo[pl.ds(first, HEAD_DIM), :], preferred_element_type=jnp.float32
            )
        return use

    oacc[...] = jnp.zeros_like(oacc)
    loads[5].wait()
    theirs(1, 1)
    combine(0)
    theirs(2, 1)
    gathers[0][1](0)
    theirs(3, 1)
    gathers[0][1](1)
    combine(1)
    gathers[0][1](2)
    gathers[0][1](3)
    gathers[1][1](0)
    for k in range(4):
        gathers[0][2](k, project_out(0))
        if k < 3:
            gathers[1][1](k + 1)
    for k in range(4):
        gathers[1][2](k, project_out(1))
    out_ref[...] = oacc[...].astype(jnp.bfloat16)
    finish_first()
    for h in range(2):
        gathers[h][3]()
    for k in range(1, 4):
        for copy in kv_copies(k):
            copy.wait_send()
    pcp(q, 0, yn).wait_send()
    pcp(q, 1, sib).wait_send()
    pcp(yq, 1, sib).wait_send()
    for t in range(1, 4):
        for h in range(2):
            for copy in part_copies(t, h, near[t], False):
                copy.wait_send()


KV_AFTER = 1


def fused_body(
    hidden_in, norm_gain, w_query, w_key, w_value, w_out, cache_keys, cache_values, offset, length
):
    tokens, depth = hidden_in.shape
    keys = cache_keys.shape[0]
    hidden = jnp.concatenate([hidden_in, jnp.broadcast_to(norm_gain, (PAD_ROWS, depth))], axis=0)
    kv = jnp.transpose(jnp.stack([cache_keys, cache_values]), (2, 0, 1, 3))
    half_dim = HEAD_DIM // 2
    inverse = ROPE_BASE ** (-(jnp.arange(half_dim, dtype=jnp.float32) * 2.0 / HEAD_DIM))
    positions = offset[0] + jnp.arange(tokens, dtype=jnp.int32)
    angles = positions.astype(jnp.float32)[:, None] * inverse[None, :]
    cosine, sine = jnp.cos(angles), jnp.sin(angles)
    cosine = jnp.concatenate([cosine, cosine], axis=1)
    sine = jnp.concatenate([-sine, sine], axis=1)
    smem = pl.BlockSpec(memory_space=pltpu.SMEM)
    vmem = pl.BlockSpec(memory_space=pltpu.VMEM)
    hbm = pl.BlockSpec(memory_space=pl.ANY)
    bf16, f32 = jnp.bfloat16, jnp.float32
    dma = pltpu.SemaphoreType.DMA
    n = FUSED_DEVICES
    return pl.pallas_call(
        fused_kernel,
        out_shape=jax.ShapeDtypeStruct((tokens, w_out.shape[1]), bf16),
        in_specs=[smem, smem, hbm, hbm, hbm, hbm, hbm, hbm, vmem, vmem],
        out_specs=vmem,
        scratch_shapes=[
            pltpu.VMEM((n, tokens + PAD_ROWS, depth), bf16),
            pltpu.VMEM(w_query.shape, bf16),
            pltpu.VMEM((64, w_query.shape[0]), bf16),
            pltpu.VMEM(w_out.shape, bf16),
            pltpu.VMEM((PLANES, keys, HEAD_DIM), bf16),
            pltpu.VMEM((PLANES, keys, HEAD_DIM), bf16),
            pltpu.VMEM((HEAD_DIM, PLANES * keys), bf16),
            pltpu.VMEM((PLANE, 320, tokens), bf16),
            pltpu.VMEM((2, HEAD_DIM, tokens), f32),
            pltpu.VMEM((2, 1, tokens), f32),
            pltpu.VMEM((2, 1, tokens), f32),
            pltpu.VMEM((8, HEAD_DIM, tokens), bf16),
            pltpu.VMEM((8, 8, tokens), f32),
            pltpu.VMEM((8, HEAD_DIM, tokens), bf16),
            pltpu.VMEM((8, 8, tokens), f32),
            pltpu.VMEM((2, n, tokens, HEAD_DIM), bf16),
            pltpu.VMEM((tokens, 128), f32),
            pltpu.VMEM((tokens, 2 * HEAD_DIM), f32),
            pltpu.VMEM((64, tokens), f32),
            pltpu.VMEM((tokens, w_out.shape[1]), f32),
            dma((n, 4)), dma((n,)),
            dma((PLANES, 2)), dma((PLANES, 2)),
            dma((PLANE, 2)), dma((PLANE,)),
            dma((4, 2, 2)), dma((4, 2, 2)),
            dma((2, n, 7)), dma((2, n)),
            dma((7,)),
        ],
        compiler_params=pltpu.CompilerParams(
            collective_id=0, has_side_effects=True, vmem_limit_bytes=50 * 1024 * 1024
        ),
        cost_estimate=pl.CostEstimate(flops=6_000_000_000, bytes_accessed=16_000_000, transcendentals=6_000_000),
    )(offset, length, hidden, w_query, w_key.T, w_value.T, w_out, kv, cosine, sine)


def solution(mesh):
    body = fused_body if mesh.shape["weight"] == FUSED_DEVICES else general_body
    return jax.shard_map(
        body,
        mesh=mesh,
        in_specs=(
            P("groups", "weight"),
            P(None, "weight"),
            P(None, "weight"),
            P(None, "weight"),
            P(None, "weight"),
            P(None, "weight"),
            P(("groups", "weight"), None, None),
            P(("groups", "weight"), None, None),
            P("groups"),
            P("groups"),
        ),
        out_specs=P("groups", "weight"),
        check_vma=False,
    )
```

```python
import functools
import math

import jax
import jax.numpy as jnp
from jax import lax
from jax.experimental import pallas as pl
from jax.experimental.pallas import tpu as pltpu
from jax.sharding import PartitionSpec as P

QHEADS = 32
KVHEADS = 4
HEAD_DIM = 128


EPSILON = 1e-05
ROPE_BASE = 500000.0
NEG_FILL = -1e30


def rotate(vectors, positions):
    half_dim = vectors.shape[-1] // 2
    inverse = ROPE_BASE ** (-(jnp.arange(half_dim, dtype=jnp.float32) * 2.0 / vectors.shape[-1]))
    angles = positions.astype(jnp.float32)[:, None] * inverse[None, :]
    cosine = jnp.cos(angles)[:, None, :]
    sine_val = jnp.sin(angles)[:, None, :]
    first = vectors[..., :half_dim]
    second = vectors[..., half_dim:]
    return jnp.concatenate(
        [first * cosine - second * sine_val, second * cosine + first * sine_val], axis=-1
    )


def general_body(
    hidden_in, norm_gain, w_query, w_key, w_value, w_out, cache_keys, cache_values, offset, length
):
    my_index = lax.axis_index("weight")
    new_rows = hidden_in.shape[0]
    gathered, gain_all = (
        lax.all_gather(hidden_in, "weight", axis=1, tiled=True),
        lax.all_gather(norm_gain, "weight", axis=1, tiled=True),
    )
    values_f = gathered.astype(jnp.float32)
    normed = (
        values_f
        * lax.rsqrt(jnp.mean(values_f * values_f, axis=1, keepdims=True) + EPSILON)
        * gain_all.astype(jnp.float32)
    ).astype(jnp.bfloat16)
    query_cols = jnp.dot(normed, w_query, preferred_element_type=jnp.float32).astype(jnp.bfloat16)
    key_cols = jnp.dot(normed, w_key, preferred_element_type=jnp.float32).astype(jnp.bfloat16)
    value_cols = jnp.dot(normed, w_value, preferred_element_type=jnp.float32).astype(jnp.bfloat16)
    queries = lax.all_gather(query_cols, "weight", axis=1, tiled=True)
    fresh = lax.all_to_all(
        jnp.stack([key_cols, value_cols]), "weight", split_axis=1, concat_axis=2, tiled=True
    )
    own_rows = fresh.shape[1]
    start = offset[0]
    query_pos = start + jnp.arange(new_rows, dtype=jnp.int32)
    queries_rot = rotate(
        queries.astype(jnp.float32).reshape(new_rows, QHEADS, HEAD_DIM), query_pos
    ).astype(jnp.bfloat16)
    fresh_index = my_index * own_rows + jnp.arange(own_rows, dtype=jnp.int32)
    keys_rot = rotate(
        fresh[0].astype(jnp.float32).reshape(own_rows, KVHEADS, HEAD_DIM), start + fresh_index
    ).astype(jnp.bfloat16)
    fresh_values = fresh[1].reshape(own_rows, KVHEADS, HEAD_DIM)
    cache_rows = cache_keys.shape[0]
    prefix_ok = my_index * cache_rows + jnp.arange(cache_rows, dtype=jnp.int32) < start
    fresh_ok = (fresh_index[None, :] <= jnp.arange(new_rows, dtype=jnp.int32)[:, None]) & (
        start + fresh_index < length[0]
    )[None, :]
    group_size = QHEADS // KVHEADS
    score_scale = 1.0 / math.sqrt(HEAD_DIM)
    peaks = []
    totals = []
    mixes = []
    for group in range(KVHEADS):
        grouped = queries_rot[:, group * group_size : (group + 1) * group_size, :]
        prefix_scores = (
            jnp.einsum(
                "tgd,kd->tgk", grouped, cache_keys[:, group, :], preferred_element_type=jnp.float32
            )
            * score_scale
        )
        prefix_scores = jnp.where(prefix_ok[None, None, :], prefix_scores, NEG_FILL)
        fresh_scores = (
            jnp.einsum(
                "tgd,kd->tgk", grouped, keys_rot[:, group, :], preferred_element_type=jnp.float32
            )
            * score_scale
        )
        fresh_scores = jnp.where(fresh_ok[:, None, :], fresh_scores, NEG_FILL)
        peak = jnp.maximum(jnp.max(prefix_scores, axis=-1), jnp.max(fresh_scores, axis=-1))
        prefix_weights = jnp.exp(prefix_scores - peak[..., None])
        fresh_weights = jnp.exp(fresh_scores - peak[..., None])
        total = jnp.sum(prefix_weights, axis=-1) + jnp.sum(fresh_weights, axis=-1)
        mixed = jnp.einsum(
            "tgk,kd->tgd",
            prefix_weights.astype(jnp.bfloat16),
            cache_values[:, group, :],
            preferred_element_type=jnp.float32,
        )
        mixed = mixed + jnp.einsum(
            "tgk,kd->tgd",
            fresh_weights.astype(jnp.bfloat16),
            fresh_values[:, group, :],
            preferred_element_type=jnp.float32,
        )
        peaks.append(peak)
        totals.append(total)
        mixes.append(mixed)
    local_peak = jnp.concatenate(peaks, axis=1)
    local_total = jnp.concatenate(totals, axis=1)
    local_mixed = jnp.concatenate(mixes, axis=1)
    global_peak = lax.pmax(local_peak.astype(jnp.bfloat16), "weight").astype(local_peak.dtype)
    factor = jnp.exp(local_peak - global_peak)
    scaled_mixed = (local_mixed * factor[..., None]).reshape(new_rows, QHEADS * HEAD_DIM)
    mixed_share = lax.psum_scatter(scaled_mixed, "weight", scatter_dimension=1, tiled=True)
    denominator = lax.psum(local_total * factor, "weight")
    share_cols = mixed_share.shape[1]
    head_of = (my_index * share_cols + jnp.arange(share_cols, dtype=jnp.int32)) // HEAD_DIM
    selector = (head_of[:, None] == jnp.arange(QHEADS, dtype=jnp.int32)[None, :]).astype(
        jnp.float32
    )
    denom_share = jnp.dot(denominator, selector.T, precision=lax.Precision.HIGHEST)
    attention_share = (mixed_share / denom_share).astype(jnp.bfloat16)
    attention = lax.all_gather(attention_share, "weight", axis=1, tiled=True)
    return jnp.dot(attention, w_out, preferred_element_type=jnp.float32).astype(jnp.bfloat16)


PLANES = 4
PLANE = 4
PAD_ROWS = 16
FUSED_DEVICES = PLANES * PLANE


def near_order(z):
    half = lax.div(z, 2)
    return [z, z + 1 - 2 * lax.rem(z, 2), 2 - half, 3 * (1 - half)]


def fused_kernel(
    start_ref, length_ref, hidden, w_query, wk_t, wv_t, w_out, kv, cos_hbm, sin_hbm,
    out_ref,
    cos_ref, sin_ref, stats, xg, wq, wkv, wo, kb, vb, vt, pq, acc, peak, total, so, sl, ro, rl, at, rinv, qacc, kacc, oacc,
    ssst, rsst, ss1, rs1, sskv, rskv, ss2, rs2, ss3, rs3, ss4, rs4, local_sem,
):
    me = lax.axis_index("weight")
    z = lax.div(me, 4)
    y = lax.rem(lax.div(me, 2), 2)
    c = lax.rem(me, 2)
    q = lax.rem(me, 4)
    plane0 = z * 4
    up, down = me + 4, me - 4
    yn = me + 2 - 4 * y
    sib = me + 1 - 2 * c
    ynsib = yn + 1 - 2 * c
    order = near_order(z)
    tokens = out_ref.shape[0]
    half = tokens // 2
    depth = xg.shape[3]
    keys = kb.shape[1]

    def remote(src, dst, ssem, rsem, dev):
        return pltpu.make_async_remote_copy(
            src_ref=src, dst_ref=dst, send_sem=ssem, recv_sem=rsem,
            device_id={"weight": dev}, device_id_type=pl.DeviceIdType.MESH,
        )

    barrier = pltpu.get_barrier_semaphore()
    for j in range(1, FUSED_DEVICES):
        pl.semaphore_signal(
            barrier, inc=1, device_id={"weight": lax.rem(me + j, FUSED_DEVICES)},
            device_id_type=pl.DeviceIdType.MESH,
        )
    own_copy = pltpu.make_async_copy(hidden, xg.at[me], local_sem.at[0])
    own_copy.start()
    own_copy.wait()
    for side in range(2):
        x = xg[me, side, 0:half, :].astype(jnp.float32)
        xx = x * x
        part = xx[:, 0:128]
        for j in range(1, depth // 128):
            part = part + xx[:, j * 128 : (j + 1) * 128]
        row_sum = jnp.sum(jnp.transpose(part), axis=0, keepdims=True)
        stats[me, :, side * half : (side + 1) * half] = jnp.broadcast_to(row_sum, (8, half))
    pl.semaphore_wait(barrier, FUSED_DEVICES - 1)

    def stat_copy(j, slot, dev):
        return remote(stats.at[slot], stats.at[slot], ssst.at[j], rsst.at[j], dev)

    for j in range(1, FUSED_DEVICES):
        stat_copy(j, me, lax.rem(me + j, FUSED_DEVICES)).start()

    def gather(slots, own, ss, rs, direct):
        def cp(i, src, d, dev):
            return remote(src, slots.at[i], ss.at[i, d], rs.at[i], dev)

        def along(i, src, first, act):
            if direct:
                if first:
                    for k in range(1, 4):
                        act(cp(i, src, 3 + k, order[k] * 4 + q))
                return
            o = lax.div(i, 4)

            @pl.when((o <= z) & (z < 3))
            def _():
                act(cp(i, src, 0, up))

            @pl.when((o >= z) & (z > 0))
            def _():
                act(cp(i, src, 1, down))

        def across(i, src, act):
            act(cp(i, src, 2, yn))
            act(cp(i, src, 3, sib))

        def begin():
            along(me, own, True, lambda copy: copy.start())
            across(me, own, lambda copy: copy.start())

        def forward(k):
            if k < 3:
                i = order[k + 1] * 4 + q
                cp(i, slots.at[i], 2, yn).wait_recv()
                along(i, slots.at[i], False, lambda copy: copy.start())
                across(i, slots.at[i], lambda copy: copy.start())
            i = order[k] * 4 + lax.rem(yn, 4)
            cp(i, slots.at[i], 2, yn).wait_recv()
            cp(i, slots.at[i], 3, sib).start()

        def last(k):
            for other in (sib, ynsib):
                i = order[k] * 4 + lax.rem(other, 4)
                cp(i, slots.at[i], 3, sib).wait_recv()

        def consume(k, use):
            use(order[k] * 4 + q)
            use(order[k] * 4 + lax.rem(yn, 4))
            last(k)
            use(order[k] * 4 + lax.rem(sib, 4))
            use(order[k] * 4 + lax.rem(ynsib, 4))

        def finish():
            along(me, own, True, lambda copy: copy.wait_send())
            across(me, own, lambda copy: copy.wait_send())
            for k in range(1, 4):
                i = order[k] * 4 + q
                along(i, slots.at[i], False, lambda copy: copy.wait_send())
                across(i, slots.at[i], lambda copy: copy.wait_send())
            for k in range(4):
                i = order[k] * 4 + lax.rem(yn, 4)
                cp(i, slots.at[i], 3, sib).wait_send()

        return begin, forward, consume, finish, last

    loads = [
        pltpu.make_async_copy(w_query, wq, local_sem.at[1]),
        pltpu.make_async_copy(wk_t, wkv.at[pl.ds(0, 32)], local_sem.at[2]),
        pltpu.make_async_copy(wv_t, wkv.at[pl.ds(32, 32)], local_sem.at[3]),
        pltpu.make_async_copy(kv.at[z, 0], kb.at[z], local_sem.at[4]),
        pltpu.make_async_copy(kv.at[z, 1], vb.at[z], local_sem.at[6]),
        pltpu.make_async_copy(w_out, wo, local_sem.at[5]),
        pltpu.make_async_copy(cos_hbm, cos_ref, local_sem.at[7]),
        pltpu.make_async_copy(sin_hbm, sin_ref, local_sem.at[8]),
    ]

    def kv_copies(k):
        o = order[k]
        return [
            remote(kv.at[o, j], buf.at[z], sskv.at[o, j], rskv.at[z, j], o * 4 + q)
            for j, buf in enumerate((kb, vb))
        ]

    def kv_arrivals(k):
        o = order[k]
        return [
            remote(kv.at[o, j], buf.at[o], sskv.at[o, j], rskv.at[o, j], o * 4 + q)
            for j, buf in enumerate((kb, vb))
        ]

    firsts = [
        gather(xg.at[:, side], hidden.at[side], ss1.at[side], rs1.at[side], False)
        for side in range(2)
    ]
    for first in firsts:
        first[0]()
    for load in loads:
        load.start()
    qacc[...] = jnp.zeros_like(qacc)
    kacc[...] = jnp.zeros_like(kacc)

    def project(i):
        x = jnp.concatenate([xg[i, side, 0:half, :] for side in range(2)], axis=0).astype(jnp.float32)
        gain = xg[i, 0, half : half + 1, :].astype(jnp.float32)
        scale = jnp.concatenate([rinv[...]] * (depth // 128), axis=1)
        normed = (x * scale * gain).astype(jnp.bfloat16)
        first = pl.multiple_of(i * depth, depth)
        qacc[...] += jnp.dot(normed, wq[pl.ds(first, depth), :], preferred_element_type=jnp.float32)
        kacc[...] += lax.dot_general(
            wkv[:, pl.ds(first, depth)], normed, (((1,), (1,)), ((), ())),
            preferred_element_type=jnp.float32,
        )

    def pair(k, one, two):
        def step(j, carry):
            project(order[k] * 4 + one + j * (two - one))
            return carry

        lax.fori_loop(0, 2, step, 0)

    def project_last(k):
        for first in firsts:
            first[4](k)
        pair(k, lax.rem(sib, 4), lax.rem(ynsib, 4))

    for k in range(4):
        for first in firsts:
            first[1](k)
        if k == KV_AFTER:
            for j in range(1, 4):
                for copy in kv_copies(j):
                    copy.start()
        if k == 0:
            for j in range(1, FUSED_DEVICES):
                sender = lax.rem(me + FUSED_DEVICES - j, FUSED_DEVICES)
                stat_copy(j, sender, sender).wait_recv()
            sums = stats[0]
            for i in range(1, FUSED_DEVICES):
                sums = sums + stats[i]
            scale_row = lax.rsqrt(sums[0:1] * (1.0 / (depth * FUSED_DEVICES)) + EPSILON)
            rinv[...] = jnp.transpose(jnp.broadcast_to(scale_row, (128, tokens)))
            for load in loads[:3]:
                load.wait()
        pair(k, q, lax.rem(yn, 4))
        if k > 0:
            project_last(k - 1)
    project_last(3)

    loads[6].wait()
    loads[7].wait()

    def turn(x):
        return x * cos_ref[...] + pltpu.roll(x, 64, 1) * sin_ref[...]

    queries = qacc[...].astype(jnp.bfloat16).astype(jnp.float32)
    for h in range(2):
        rows = slice(h * HEAD_DIM, (h + 1) * HEAD_DIM)
        pq[q, rows, :] = jnp.transpose(turn(queries[:, rows])).astype(jnp.bfloat16)
    pq[q, 256:320, :] = kacc[...].astype(jnp.bfloat16)

    def pcp(i, d, dev):
        return remote(pq.at[i], pq.at[i], ss2.at[i, d], rs2.at[i], dev)

    yq, sq, ysq = lax.rem(yn, 4), lax.rem(sib, 4), lax.rem(ynsib, 4)
    near = [q, yq, ysq, sq]
    pcp(q, 0, yn).start()
    pcp(q, 1, sib).start()

    loads[3].wait()
    loads[4].wait()
    start = start_ref[0]
    length = length_ref[0]
    score_scale = math.log2(math.e) / math.sqrt(HEAD_DIM)

    def attend(query, blocks, top=None, whole=None, mixed=None):
        for key_rows, value_cols, allowed in blocks:
            scores = jnp.dot(key_rows, query, preferred_element_type=jnp.float32) * score_scale
            if allowed is not None:
                scores = jnp.where(allowed, scores, NEG_FILL)
            new = jnp.max(scores, axis=0, keepdims=True)
            if top is not None:
                new = jnp.maximum(top, new)
            weights = jnp.exp2(scores - new)
            part = jnp.sum(weights, axis=0, keepdims=True)
            product = jnp.dot(
                value_cols, weights.astype(jnp.bfloat16), preferred_element_type=jnp.float32
            )
            if top is not None:
                factor = jnp.exp2(top - new)
                part = part + whole * factor
                product = product + mixed * factor
            top, whole, mixed = new, part, product
        return top, whole, mixed

    def cache_blocks():
        row = lax.broadcasted_iota(jnp.int32, (keys, tokens), 0)
        last = row < start - ((PLANES - 1) * 4 + q) * keys
        return [
            (kb[o], vt[o], last if o == PLANES - 1 else None)
            for o in range(PLANES)
        ]

    def head_rows(h):
        if isinstance(h, int):
            return pl.ds(h * HEAD_DIM, HEAD_DIM)
        return pl.ds(pl.multiple_of(h * HEAD_DIM, HEAD_DIM), HEAD_DIM)

    def keep(n, result):
        top, whole, mixed = result
        so[n] = (mixed * (1.0 / whole)).astype(jnp.bfloat16)
        sl[n, 0:1, :] = top + jnp.log2(whole)
        sl[n, 1:8, :] = jnp.zeros((7, tokens), jnp.float32)

    def mine(k, o):
        row = lax.broadcasted_iota(jnp.int32, (keys, tokens), 0)
        allowed = row < start - (o * 4 + q) * keys

        def one(h, carry):
            before = () if k == 0 else (peak[h], total[h], acc[h])
            peak[h], total[h], acc[h] = attend(
                pq[q, head_rows(h), :], [(kb[o], vt[o], allowed)], *before
            )
            return carry

        lax.fori_loop(0, 2, one, 0)

    for k in range(4):
        o = order[k]
        if k > 0:
            for copy in kv_arrivals(k):
                copy.wait_recv()
        vt[o] = jnp.transpose(vb[o])
        if k == 3:
            pcp(yq, 0, yn).wait_recv()
            pcp(yq, 1, sib).start()
        mine(k, o)

    pcp(sq, 1, sib).wait_recv()

    def part_copies(t, h, p, back):
        n = p * 2 + h
        m = q * 2 + h
        target = n if back else m
        return [
            remote(so.at[n], ro.at[target], ss3.at[t, h, 0], rs3.at[t, h, 0], plane0 + p),
            remote(sl.at[n], rl.at[target], ss3.at[t, h, 1], rs3.at[t, h, 1], plane0 + p),
        ]

    def theirs(t, h):
        p = near[t]
        keep(p * 2 + h, attend(pq[p, head_rows(h), :], cache_blocks()))
        for copy in part_copies(t, h, p, False):
            copy.start()

    theirs(1, 0)
    pcp(ysq, 1, sib).wait_recv()
    fresh_key = jnp.transpose(
        jnp.concatenate([pq[p, 256:288, :] for p in range(PLANE)], axis=0).astype(jnp.float32)
    )
    fresh_key = turn(fresh_key).astype(jnp.bfloat16)
    fresh_value = jnp.concatenate([pq[p, 288:320, :] for p in range(PLANE)], axis=0)
    row = lax.broadcasted_iota(jnp.int32, (tokens, tokens), 0)
    token = lax.broadcasted_iota(jnp.int32, (tokens, tokens), 1)
    fresh_ok = (row <= token) & (row < length - start)
    for h in range(2):
        top, whole, mixed = attend(
            pq[q, head_rows(h), :], [(fresh_key, fresh_value, fresh_ok)]
        )
        new = jnp.maximum(top, peak[h])
        one, two = jnp.exp2(top - new), jnp.exp2(peak[h] - new)
        keep(q * 2 + h, (new, whole * one + total[h] * two, mixed * one + acc[h] * two))
    theirs(2, 0)
    theirs(3, 0)

    gathers = [gather(at.at[h], at.at[h, me], ss4.at[h], rs4.at[h], True) for h in range(2)]

    def combine(h):
        for t in range(1, 4):
            for copy in part_copies(t, h, near[t], True):
                copy.wait_recv()
        lses = [sl[q * 2 + h, 0:1, :]] + [rl[near[t] * 2 + h, 0:1, :] for t in range(1, 4)]
        parts = [so[q * 2 + h]] + [ro[near[t] * 2 + h] for t in range(1, 4)]
        top = jnp.maximum(jnp.maximum(lses[0], lses[1]), jnp.maximum(lses[2], lses[3]))
        shares = [jnp.exp2(lse - top) for lse in lses]
        whole = shares[0] + shares[1] + shares[2] + shares[3]
        mixed = sum(part.astype(jnp.float32) * share for part, share in zip(parts, shares)) / whole
        at[h, me] = jnp.transpose(mixed).astype(jnp.bfloat16)
        gathers[h][0]()

    def project_out(h):
        def use(i):
            first = pl.multiple_of((i * 2 + h) * HEAD_DIM, HEAD_DIM)
            oacc[...] += jnp.dot(
                at[h, i], wo[pl.ds(first, HEAD_DIM), :], preferred_element_type=jnp.float32
            )
        return use

    oacc[...] = jnp.zeros_like(oacc)
    loads[5].wait()
    theirs(1, 1)
    combine(0)
    theirs(2, 1)
    gathers[0][1](0)
    theirs(3, 1)
    gathers[0][1](1)
    combine(1)
    gathers[0][1](2)
    gathers[0][1](3)
    gathers[1][1](0)
    for k in range(4):
        gathers[0][2](k, project_out(0))
        if k < 3:
            gathers[1][1](k + 1)
    for k in range(4):
        gathers[1][2](k, project_out(1))
    out_ref[...] = oacc[...].astype(jnp.bfloat16)
    for first in firsts:
        first[3]()
    for j in range(1, FUSED_DEVICES):
        stat_copy(j, me, lax.rem(me + j, FUSED_DEVICES)).wait_send()
    for h in range(2):
        gathers[h][3]()
    for k in range(1, 4):
        for copy in kv_copies(k):
            copy.wait_send()
    pcp(q, 0, yn).wait_send()
    pcp(q, 1, sib).wait_send()
    pcp(yq, 1, sib).wait_send()
    for t in range(1, 4):
        for h in range(2):
            for copy in part_copies(t, h, near[t], False):
                copy.wait_send()


KV_AFTER = 1


def fused_body(
    hidden_in, norm_gain, w_query, w_key, w_value, w_out, cache_keys, cache_values, offset, length
):
    tokens, depth = hidden_in.shape
    keys = cache_keys.shape[0]
    halves = hidden_in.reshape(2, tokens // 2, depth)
    hidden = jnp.concatenate([halves, jnp.broadcast_to(norm_gain, (2, PAD_ROWS, depth))], axis=1)
    kv = jnp.transpose(jnp.stack([cache_keys, cache_values]), (2, 0, 1, 3))
    half_dim = HEAD_DIM // 2
    inverse = ROPE_BASE ** (-(jnp.arange(half_dim, dtype=jnp.float32) * 2.0 / HEAD_DIM))
    positions = offset[0] + jnp.arange(tokens, dtype=jnp.int32)
    angles = positions.astype(jnp.float32)[:, None] * inverse[None, :]
    cosine, sine = jnp.cos(angles), jnp.sin(angles)
    cosine = jnp.concatenate([cosine, cosine], axis=1)
    sine = jnp.concatenate([-sine, sine], axis=1)
    smem = pl.BlockSpec(memory_space=pltpu.SMEM)
    vmem = pl.BlockSpec(memory_space=pltpu.VMEM)
    hbm = pl.BlockSpec(memory_space=pl.ANY)
    bf16, f32 = jnp.bfloat16, jnp.float32
    dma = pltpu.SemaphoreType.DMA
    n = FUSED_DEVICES
    return pl.pallas_call(
        fused_kernel,
        out_shape=jax.ShapeDtypeStruct((tokens, w_out.shape[1]), bf16),
        in_specs=[smem, smem, hbm, hbm, hbm, hbm, hbm, hbm, hbm, hbm],
        out_specs=vmem,
        scratch_shapes=[
            pltpu.VMEM((tokens, HEAD_DIM), f32),
            pltpu.VMEM((tokens, HEAD_DIM), f32),
            pltpu.VMEM((n, 8, tokens), f32),
            pltpu.VMEM((n, 2, tokens // 2 + PAD_ROWS, depth), bf16),
            pltpu.VMEM(w_query.shape, bf16),
            pltpu.VMEM((64, w_query.shape[0]), bf16),
            pltpu.VMEM(w_out.shape, bf16),
            pltpu.VMEM((PLANES, keys, HEAD_DIM), bf16),
            pltpu.VMEM((PLANES, keys, HEAD_DIM), bf16),
            pltpu.VMEM((PLANES, HEAD_DIM, keys), bf16),
            pltpu.VMEM((PLANE, 320, tokens), bf16),
            pltpu.VMEM((2, HEAD_DIM, tokens), f32),
            pltpu.VMEM((2, 1, tokens), f32),
            pltpu.VMEM((2, 1, tokens), f32),
            pltpu.VMEM((8, HEAD_DIM, tokens), bf16),
            pltpu.VMEM((8, 8, tokens), f32),
            pltpu.VMEM((8, HEAD_DIM, tokens), bf16),
            pltpu.VMEM((8, 8, tokens), f32),
            pltpu.VMEM((2, n, tokens, HEAD_DIM), bf16),
            pltpu.VMEM((tokens, 128), f32),
            pltpu.VMEM((tokens, 2 * HEAD_DIM), f32),
            pltpu.VMEM((64, tokens), f32),
            pltpu.VMEM((tokens, w_out.shape[1]), f32),
            dma((n,)), dma((n,)),
            dma((2, n, 4)), dma((2, n)),
            dma((PLANES, 2)), dma((PLANES, 2)),
            dma((PLANE, 2)), dma((PLANE,)),
            dma((4, 2, 2)), dma((4, 2, 2)),
            dma((2, n, 7)), dma((2, n)),
            dma((9,)),
        ],
        compiler_params=pltpu.CompilerParams(
            collective_id=0, has_side_effects=True, vmem_limit_bytes=50 * 1024 * 1024
        ),
        cost_estimate=pl.CostEstimate(flops=6_000_000_000, bytes_accessed=16_000_000, transcendentals=6_000_000),
    )(offset, length, hidden, w_query, w_key.T, w_value.T, w_out, kv, cosine, sine)


def solution(mesh):
    body = fused_body if mesh.shape["weight"] == FUSED_DEVICES else general_body
    return jax.shard_map(
        body,
        mesh=mesh,
        in_specs=(
            P("groups", "weight"),
            P(None, "weight"),
            P(None, "weight"),
            P(None, "weight"),
            P(None, "weight"),
            P(None, "weight"),
            P(("groups", "weight"), None, None),
            P(("groups", "weight"), None, None),
            P("groups"),
            P("groups"),
        ),
        out_specs=P("groups", "weight"),
        check_vma=False,
    )
```
